32 devices in a mesh: dp: 4 (over y, core), slab: 8 (over z, x).
Axes of the slice: x: 2, y: 2, z: 4, core: 2. Of those that a mesh axis runs over, the one named last changes fastest.
Arguments:
- features: bfloat16 [4, 80, 64, 256], P('dp', 'slab'), may hold values from -6 to 6
- cotangent: bfloat16 [4, 80, 64, 256], P('dp', 'slab'), may hold values from -6 to 6
- neighbour_table: int32 [4, 80, 27], P('dp', 'slab'), may hold values from 0 to 14, as said below
- send_lists: int32 [4, 8, 2, 2], P('dp', 'slab'), may hold values from 0 to 10, as said below
- block_counts: int32 [4, 8], P('dp', 'slab'), may hold values from 5 to 10, as said below
- weight_one: bfloat16 [6912, 256], replicated, may hold values from -0.078125 to 0.078125
- weight_two: bfloat16 [6912, 256], replicated, may hold values from -0.078125 to 0.078125
Outputs:
- output: bfloat16 [4, 80, 64, 256], P('dp', 'slab')
- grad_features: bfloat16 [4, 80, 64, 256], P('dp', 'slab')
- grad_one: float32 [6912, 256], P('slab', 'dp')
- grad_two: float32 [6912, 256], P('slab', 'dp')
The draws below stay inside these ranges and needn't reach their ends.
Inputs may be any that keep to these rules, and one draw needn't show every extreme that they name: `neighbour_table`: row b of slab l = b // 10 lists where the block at each of the 27 block offsets lies, in the numbering of the gathered step; rows of padding slots hold only 14. The relation is symmetric: a block that names another at an offset is named by it at the opposite offset. `send_lists`: list 0 of a slab names, in increasing order, its occupied blocks in its first block-plane, the ones the previous slab can touch; list 1 those of its last block-plane; 10 fills the remaining slots. `block_counts`: slots at and above a slab's count are padding.
All inputs are finite; a program needn't handle non-finite values.
Results may differ from the reference program's by a relative error of at most 0.013.
Values may be sent and summed in bfloat16 or wider, within the bound.
No kernel may reach another device: no remote copies, remote signals or barrier semaphores. Data moves between devices by JAX's collectives and lax.ppermute only.
A program may use at most 128 MiB of HBM per device.

```python
import math
import jax
import jax.numpy as jnp
from jax import lax

WIDTH = 256
GRID_X = 5
GRID_Y = 2
GRID_Z = 2
SLAB_BLOCKS = 10
EDGE = 2
TAPS_IN = 6912
SCENES = 4
SLABS = 8
BLOCKS = 80


def slab_layout(key, filled, sparse):
    plane_size = GRID_Y * GRID_Z
    plane_half = plane_size // 2
    key_counts, key_order = jax.random.split(key)
    per_plane = jax.random.randint(key_counts, (GRID_X,), 1, plane_half + 1).astype(jnp.int32)
    per_plane = jnp.where(sparse, per_plane.at[0].set(1), per_plane)
    per_plane = jnp.where(filled, jnp.full((GRID_X,), plane_half, jnp.int32), per_plane)

    def order_of(sub_key):
        return jax.random.permutation(sub_key, plane_size)
    orders = jax.vmap(order_of)(jax.random.split(key_order, GRID_X))
    ranking = jnp.argsort(orders, axis=1)
    occupied = ranking < per_plane[:, None]
    marked = occupied.reshape(-1).astype(jnp.int32)
    running = (jnp.cumsum(marked) - 1).astype(jnp.int32)
    index_of = jnp.where(marked > 0, running, -1).astype(jnp.int32)
    first_rank = (jnp.cumsum(occupied[0].astype(jnp.int32)) - 1).astype(jnp.int32)
    last_rank = (jnp.cumsum(occupied[GRID_X - 1].astype(jnp.int32)) - 1).astype(jnp.int32)
    places = jnp.arange(plane_size)
    list_first = jnp.full((EDGE + 1,), SLAB_BLOCKS, jnp.int32).at[jnp.where(occupied[0], first_rank, EDGE)].set(index_of[places])[:EDGE]
    list_last = jnp.full((EDGE + 1,), SLAB_BLOCKS, jnp.int32).at[jnp.where(occupied[GRID_X - 1], last_rank, EDGE)].set(index_of[(GRID_X - 1) * plane_size + places])[:EDGE]
    position = jnp.zeros((SLAB_BLOCKS + 1,), jnp.int32).at[jnp.where(marked > 0, running, SLAB_BLOCKS)].set(jnp.arange(GRID_X * plane_size, dtype=jnp.int32))[:SLAB_BLOCKS]
    filled_count = jnp.sum(marked).astype(jnp.int32)
    return (occupied, index_of, first_rank, last_rank, jnp.stack([list_first, list_last]), position, filled_count)


def slab_table(mine, before, after, has_before, has_after):
    plane_size = GRID_Y * GRID_Z
    index_of = mine[1]
    position = mine[5]
    filled_count = mine[6]
    offsets = jnp.arange(27)
    step_x = offsets // 9 - 1
    step_y = offsets // 3 % 3 - 1
    step_z = offsets % 3 - 1
    cell_x = position // plane_size
    cell_y = position % plane_size // GRID_Z
    cell_z = position % GRID_Z
    near_x = cell_x[:, None] + step_x[None, :]
    near_y = cell_y[:, None] + step_y[None, :]
    near_z = cell_z[:, None] + step_z[None, :]
    inside = (near_y >= 0) & (near_y < GRID_Y) & (near_z >= 0) & (near_z < GRID_Z)
    place = jnp.clip(near_y, 0, GRID_Y - 1) * GRID_Z + jnp.clip(near_z, 0, GRID_Z - 1)
    local_value = index_of[jnp.clip(near_x, 0, GRID_X - 1) * plane_size + place]
    is_local = (near_x >= 0) & (near_x < GRID_X) & (local_value >= 0)
    from_before = (near_x == -1) & has_before & before[0][GRID_X - 1][place]
    from_after = (near_x == GRID_X) & has_after & after[0][0][place]
    nothing = SLAB_BLOCKS + 2 * EDGE
    result = jnp.where(inside & is_local, local_value, jnp.where(inside & from_before, SLAB_BLOCKS + before[3][place], jnp.where(inside & from_after, SLAB_BLOCKS + EDGE + after[2][place], nothing)))
    live = jnp.arange(SLAB_BLOCKS)[:, None] < filled_count
    return jnp.where(live, result, nothing).astype(jnp.int32)


def geometry(key):
    base = jax.random.fold_in(key, 4321)

    def one_scene(scene_id):
        scene_key = jax.random.fold_in(base, scene_id)
        chosen = jax.random.randint(jax.random.fold_in(scene_key, 0), (), 0, SLABS)
        slab_ids = jnp.arange(SLABS)

        def layout_of(slab_id):
            return slab_layout(jax.random.fold_in(scene_key, slab_id + 1), slab_id == chosen, slab_id == (chosen + 1) % SLABS)
        layouts = jax.vmap(layout_of)(slab_ids)
        before = jax.tree.map(lambda leaf: jnp.roll(leaf, 1, axis=0), layouts)
        after = jax.tree.map(lambda leaf: jnp.roll(leaf, -1, axis=0), layouts)
        tables = jax.vmap(slab_table)(layouts, before, after, slab_ids > 0, slab_ids < SLABS - 1)
        return (layouts[6], tables, layouts[4])
    return jax.vmap(one_scene)(jnp.arange(SCENES))


def draw_neighbour_table(key, part):
    counts, tables, lists = geometry(key)
    return tables.reshape(SCENES, BLOCKS, 27).astype(jnp.int32)


def draw_send_lists(key, part):
    counts, tables, lists = geometry(key)
    return lists.astype(jnp.int32)


def draw_block_counts(key, part):
    counts, tables, lists = geometry(key)
    return counts.astype(jnp.int32)


def spiked(entries, stream_key, source, target, blocks, factor):
    owner, partner = [(jnp.arange(entries.shape[axis_at]) // (entries.shape[axis_at] // blocks)).reshape([-1 if axis == axis_at else 1 for axis in range(entries.ndim)]) for axis_at in (source, target)]
    chosen = jax.random.permutation(stream_key, blocks)[partner]
    strong = (owner == chosen) | (owner == (partner + blocks // 2) % blocks)
    return jnp.where(strong, factor * entries, entries)


def level_of(rng, shape, shards, low, top_value):
    def one(axis_at, shards_of):
        heights = jax.random.uniform(jax.random.fold_in(jax.random.fold_in(rng, 6), axis_at), (shards_of,), jnp.float32, low / len(shards), top_value / len(shards))
        return jnp.repeat(jnp.exp(heights), shape[axis_at] // shards_of).reshape((-1,) + (1,) * (len(shape) - axis_at - 1))

    gain = one(*shards[0])
    for cut in shards[1:]:
        gain = gain * one(*cut)
    return gain


def normal_values(rng, dims, deviation, reach, cuts=(), held_as=jnp.bfloat16):
    drawn = deviation * jax.random.normal(rng, dims, jnp.float32)
    if cuts:
        drawn = drawn * level_of(rng, dims, cuts, -0.22, 0.18)
    return jnp.clip(drawn, -reach, reach).astype(held_as)


def gaussian_with(rng, shape, spread, bound, cuts, heavy, kind=jnp.bfloat16):
    array = spread * jax.random.normal(rng, shape, jnp.float32)
    if cuts:
        array = array * level_of(rng, shape, cuts, -0.22, 0.18)
    return jnp.clip(spiked(array, jax.random.fold_in(rng, 3), *heavy), -bound, bound).astype(kind)


def setup_inputs(seed: int = 0) -> dict:
    arg_keys = jax.random.split(jax.random.key(seed), 8)
    return {
        "features": normal_values(arg_keys[0], (SCENES, BLOCKS, 64, WIDTH), 1.0, 6.0, ((0, 4), (1, 8))),
        "cotangent": gaussian_with(arg_keys[1], (SCENES, BLOCKS, 64, WIDTH), 1.0, 6.0, ((0, 4), (1, 8)), (0, 3, 4, 2.0)),
        "neighbour_table": draw_neighbour_table(jax.random.fold_in(arg_keys[7], 71), 0),
        "send_lists": draw_send_lists(jax.random.fold_in(arg_keys[7], 71), 0),
        "block_counts": draw_block_counts(jax.random.fold_in(arg_keys[7], 71), 0),
        "weight_one": normal_values(arg_keys[5], (TAPS_IN, WIDTH), TAPS_IN ** -0.5, 0.078125),
        "weight_two": normal_values(arg_keys[6], (TAPS_IN, WIDTH), TAPS_IN ** -0.5, 0.078125),
    }


OFFSET_LIST = [(along_x, along_y, along_z) for along_x in range(3) for along_y in range(3) for along_z in range(3)]

def columns(extended, lookup):
    blocks = lookup.shape[0]
    channels = extended.shape[-1]
    nearby = extended[lookup].reshape(blocks, 3, 3, 3, 4, 4, 4, channels)
    nearby = nearby.transpose(0, 1, 4, 2, 5, 3, 6, 7).reshape(blocks, 12, 12, 12, channels)
    window = nearby[:, 3:9, 3:9, 3:9]
    pieces = [window[:, along_x:along_x + 4, along_y:along_y + 4, along_z:along_z + 4].reshape(blocks * 64, channels) for along_x, along_y, along_z in OFFSET_LIST]
    return jnp.concatenate(pieces, axis=1)

def flipped(weight):
    channels = weight.shape[1]
    return jnp.transpose(weight.reshape(27, channels, channels)[::-1], (0, 2, 1)).reshape(27 * channels, channels)

def extend_all(source, edge_lists):
    slabs = source.shape[0]
    channels = source.shape[-1]
    edges = edge_lists.shape[-1]
    zero_one = jnp.zeros((slabs, 1, 64, channels), source.dtype)
    padded = jnp.concatenate([source, zero_one], axis=1)

    def pick(slab_rows, slab_lists):
        return slab_rows[slab_lists]
    picked = jax.vmap(pick)(padded, edge_lists)
    empty_edge = jnp.zeros((1, edges, 64, channels), source.dtype)
    from_prev = jnp.concatenate([empty_edge, picked[:-1, 1]], axis=0)
    from_next = jnp.concatenate([picked[1:, 0], empty_edge], axis=0)
    return jnp.concatenate([source, from_prev, from_next, zero_one], axis=1)

def reference(features, cotangent, neighbour_table, send_lists, block_counts, weight_one, weight_two):
    width_all = weight_one.shape[0]
    channels = weight_one.shape[1]
    contract = (((0,), (0,)), ((), ()))

    def scene_pass(totals, scene):
        scene_feat, scene_cot, lookup, edge_lists, counts = scene
        slabs = edge_lists.shape[0]
        blocks = scene_feat.shape[0] // slabs
        present = (jnp.arange(blocks)[None, :] < counts[:, None]).astype(jnp.float32)[:, :, None, None]
        masked = (scene_feat.reshape(slabs, blocks, 64, channels).astype(jnp.float32) * present).astype(jnp.bfloat16)
        upstream = scene_cot.reshape(slabs, blocks, 64, channels)
        lookups = lookup.reshape(slabs, blocks, 27)

        def gathered(source):
            extended = extend_all(source, edge_lists)
            return jax.vmap(columns)(extended, lookups).reshape(slabs * blocks * 64, 27 * channels)
        cols_in = gathered(masked)
        pre_one = jnp.dot(cols_in, weight_one, preferred_element_type=jnp.float32)
        hidden = jnp.maximum(pre_one, 0.0).astype(jnp.bfloat16)
        cols_hidden = gathered(hidden.reshape(slabs, blocks, 64, channels))
        pre_two = jnp.dot(cols_hidden, weight_two, preferred_element_type=jnp.float32)
        output = (pre_two + masked.reshape(-1, channels).astype(jnp.float32)).astype(jnp.bfloat16)
        back_hidden = jnp.dot(gathered(upstream), flipped(weight_two), preferred_element_type=jnp.float32)
        grad_hidden = jnp.where(hidden > 0, back_hidden, 0.0).astype(jnp.bfloat16)
        back_in = jnp.dot(gathered(grad_hidden.reshape(slabs, blocks, 64, channels)), flipped(weight_one), preferred_element_type=jnp.float32)
        rows_present = jnp.broadcast_to(present, (slabs, blocks, 64, 1)).reshape(-1, 1)
        upstream_rows = upstream.reshape(-1, channels)
        grad_features = ((upstream_rows.astype(jnp.float32) + back_in) * rows_present).astype(jnp.bfloat16)
        sum_two = lax.dot_general(cols_hidden, upstream_rows, contract, preferred_element_type=jnp.float32)
        sum_one = lax.dot_general(cols_in, grad_hidden, contract, preferred_element_type=jnp.float32)
        shaped = (output.reshape(slabs * blocks, 64, channels), grad_features.reshape(slabs * blocks, 64, channels))
        return ((totals[0] + sum_one, totals[1] + sum_two), shaped)
    empty_sum = jnp.zeros((width_all, channels), jnp.float32)
    totals, results = lax.scan(scene_pass, (empty_sum, empty_sum), (features, cotangent, neighbour_table, send_lists, block_counts))
    factor = 1.0 / math.sqrt(SCENES * SLABS * SLAB_BLOCKS * 64)
    return (results[0], results[1], totals[0] * factor, totals[1] * factor)
```

```python
import functools
import math

import jax
import jax.numpy as jnp
import numpy as np
from jax import lax
from jax.experimental import pallas as pl
from jax.experimental.pallas import tpu as pltpu
from jax.sharding import PartitionSpec as P

F32 = jnp.float32
BF16 = jnp.bfloat16
TAPS = 27
ROWS = 16
VMEM_LIMIT = 40 * 2**20

PORTIONS = {
    "two": ((0, 432, ("y", "x", "z1", "z2")),),
    "one": ((0, 432, ("x", "y", "z1", "z2")),),
}


def shift_matrix():
    out = np.zeros((9 * ROWS, 9 * ROWS), np.float32)
    for shift in range(9):
        for spot in range(ROWS):
            y = spot // 4 + shift // 3 - 1
            z = spot % 4 + shift % 3 - 1
            source = 3 * (y // 4 + 1) + z // 4 + 1
            out[shift * ROWS + spot, source * ROWS + 4 * (y % 4) + z % 4] = 1.0
    return out


def bit_of(name, dp_index, slab_index):
    if name == "y":
        return dp_index // 2
    if name == "x":
        return slab_index % 2
    if name == "z1":
        return slab_index // 2 % 2
    return slab_index // 4


def pair_perm(name, dp_size, slab_size):
    dp_flip = {"core": 1, "y": 2}.get(name, 0)
    slab_flip = {"x": 1, "z1": 2, "z2": 4}.get(name, 0)
    return [
        (d * slab_size + s, (d ^ dp_flip) * slab_size + (s ^ slab_flip))
        for d in range(dp_size)
        for s in range(slab_size)
    ]


def swap(array, name):
    dp_size, slab_size = lax.axis_size("dp"), lax.axis_size("slab")
    return lax.ppermute(array, ("dp", "slab"), pair_perm(name, dp_size, slab_size))


def swap_halos(first, second):
    count = lax.axis_size("slab")
    even = [(s, s ^ 1) for s in range(count) if s ^ 1 < count]
    odd = [(s, s + 1 if s % 2 else s - 1) for s in range(1, count) if s % 2 == 0 or s + 1 < count]
    return lax.ppermute(first, "slab", even), lax.ppermute(second, "slab", odd)


def plane_rows(x, block, blocks):
    start = (x * blocks + block) * ROWS
    return pl.ds(start if isinstance(start, int) else pl.multiple_of(start, ROWS), ROWS)


def pack_kernel(lists, features, cotangent, first, second, edges, sems):
    blocks, channels = features.shape[1], features.shape[3]
    count = lists.shape[3]
    copies = []
    for side in range(2):
        for q in range(count):
            block = jnp.minimum(lists[0, 0, side, q], blocks - 1)
            for part, source in enumerate((features, cotangent)):
                copy = pltpu.make_async_copy(
                    source.at[0, block, pl.ds(48 * side, ROWS), :],
                    edges.at[side, q, :, pl.ds(part * channels, channels)],
                    sems.at[side, q, part],
                )
                copy.start()
                copies.append(copy)
    for copy in copies:
        copy.wait()
    odd = lax.rem(lax.axis_index("slab"), 2)
    for side in range(2):
        for q in range(count):
            value = edges[side, q]
            value = jnp.where(lists[0, 0, side, q] < blocks, value, jnp.zeros_like(value))
            edges[side, q] = value
    first[...] = edges[1 - odd]
    second[...] = edges[odd]


def fill_planes(planes, own, own_blocks, got_first, got_second, lanes):
    blocks = own_blocks
    edge = got_first.shape[0]
    slots = blocks + 2 * edge + 1
    for x in range(4):
        for b in range(blocks):
            planes[plane_rows(x, b, slots), :] = own(x, b)
        planes[pl.ds((x * slots + blocks) * ROWS, (2 * edge + 1) * ROWS), :] = jnp.zeros(
            ((2 * edge + 1) * ROWS, planes.shape[1]), planes.dtype
        )
    is_odd = lax.rem(lax.axis_index("slab"), 2) == 1
    for q in range(edge):
        one, two = got_first[q, :, lanes], got_second[q, :, lanes]
        planes[plane_rows(3, blocks + q, slots), :] = jnp.where(is_odd, one, two)
        planes[plane_rows(0, blocks + edge + q, slots), :] = jnp.where(is_odd, two, one)


def gather_shifts(shifted, planes, table, shift, blocks, slots):
    matrix = shift[...]
    step = blocks * ROWS

    def one_block(b, carry):
        for at in range(6):
            near_x = 0 if at == 0 else 2 if at == 5 else 1
            x = (at - 1) % 4
            around = [
                planes[plane_rows(x, table[0, b, 9 * near_x + n], slots), :] for n in range(9)
            ]
            moved = jnp.dot(
                matrix, jnp.concatenate(around, axis=0), preferred_element_type=F32
            ).astype(BF16)
            for n in range(9):
                start = (n * 6 + at) * step + b * ROWS
                shifted[pl.ds(pl.multiple_of(start, ROWS), ROWS), :] = moved[
                    n * ROWS : (n + 1) * ROWS
                ]
        return carry

    lax.fori_loop(0, blocks, one_block, 0)


def taps_of(shifted, offset, blocks):
    along_x, along_yz = offset // 9, offset % 9
    start = (along_yz * 6 + along_x) * blocks * ROWS
    return shifted[start : start + 4 * blocks * ROWS, :]


def convolve(total, shifted, weight, blocks, flipped):
    channels = total.shape[1]
    for offset in range(TAPS):
        row = (TAPS - 1 - offset if flipped else offset) * channels
        term = lax.dot_general(
            taps_of(shifted, offset, blocks),
            weight[row : row + channels, :],
            (((1,), (1 if flipped else 0,)), ((), ())),
            preferred_element_type=F32,
        )
        if offset == 0:
            total[...] = term
        else:
            total[...] += term


def emit_share(grad, dest, portions, outs, tile_rows, slab_size):
    half = tile_rows // 2
    dp_index, slab_index = lax.axis_index("dp"), lax.axis_index("slab")
    core = lax.rem(dp_index, 2)
    lane = lax.broadcasted_iota(jnp.int32, (half, 128), 1)
    low = (lane < 64) == (core == 0)
    for y in range(2):
        upper = grad[dest * tile_rows : dest * tile_rows + half, y * 128 : (y + 1) * 128]
        lower = grad[dest * tile_rows + half : (dest + 1) * tile_rows, y * 128 : (y + 1) * 128]
        lower = pltpu.roll(lower, 64, 1)
        keep = jnp.where(low, upper, lower).astype(BF16)
        send = jnp.where(low, lower, upper).astype(BF16)
        for (first, last, order), (keep_ref, send_ref) in zip(portions, outs):
            index = 0
            for name in order:
                bit = bit_of(name, dp_index, slab_index)
                mine = y if name == "y" else bit_of(name, 0, dest)
                index = index * 2 + (bit ^ mine)
            keep_ref[index] = keep[first:last]
            send_ref[index] = send[first:last]


def emit_gradient(product, grad, portions, outs, packed):
    channels = grad.shape[1]
    if not packed:
        for offset in range(TAPS):
            outs[0][offset * channels : (offset + 1) * channels, :] = product(offset)
        return
    slab_size = packed
    tile_rows = TAPS * channels // slab_size
    done = 0
    for offset in range(TAPS):
        grad[offset * channels : (offset + 1) * channels, :] = product(offset)
        while done < slab_size and (done + 1) * tile_rows <= (offset + 1) * channels:
            emit_share(grad, done, portions, outs, tile_rows, slab_size)
            done += 1


def over_voxels(left, right):
    return lax.dot_general(left, right, (((0,), (0,)), ((), ())), preferred_element_type=F32)


def pair_up(refs, packed):
    return list(zip(refs[0::2], refs[1::2])) if packed else list(refs)


def forward_kernel(
    packed, portions, table, features, cotangent, got_first, got_second, shift, weight, hidden, *rest
):
    *outs, planes, shifted, held, total, grad, sem = rest
    outs = pair_up(outs, packed)
    blocks, channels = features.shape[1], features.shape[3]
    slots = planes.shape[0] // (4 * ROWS)
    fetch = pltpu.make_async_copy(weight, held, sem)
    fetch.start()
    fill_planes(
        planes,
        lambda x, b: features[0, b, x * ROWS : (x + 1) * ROWS, :],
        blocks,
        got_first,
        got_second,
        pl.ds(0, channels),
    )
    gather_shifts(shifted, planes, table, shift, blocks, slots)
    fetch.wait()
    convolve(total, shifted, held, blocks, False)
    hidden[...] = jnp.maximum(total[...], 0.0).astype(BF16)
    fill_planes(
        planes,
        lambda x, b: cotangent[0, b, x * ROWS : (x + 1) * ROWS, :],
        blocks,
        got_first,
        got_second,
        pl.ds(channels, channels),
    )
    gather_shifts(shifted, planes, table, shift, blocks, slots)
    emit_gradient(
        lambda offset: over_voxels(hidden[...], taps_of(shifted, TAPS - 1 - offset, blocks)),
        grad,
        portions,
        outs,
        packed,
    )


def backward_kernel(
    packed,
    portions,
    table,
    lists,
    features,
    cotangent,
    got_first,
    got_second,
    shift,
    weight,
    hidden,
    grad_hidden,
    first,
    second,
    *rest,
):
    *outs, planes, shifted, held, total, grad, sem = rest
    outs = pair_up(outs, packed)
    blocks, channels = features.shape[1], features.shape[3]
    slots = planes.shape[0] // (4 * ROWS)
    fetch = pltpu.make_async_copy(weight, held, sem)
    fetch.start()
    fill_planes(
        planes,
        lambda x, b: cotangent[0, b, x * ROWS : (x + 1) * ROWS, :],
        blocks,
        got_first,
        got_second,
        pl.ds(channels, channels),
    )
    gather_shifts(shifted, planes, table, shift, blocks, slots)
    fetch.wait()
    convolve(total, shifted, held, blocks, True)
    grad_hidden[...] = jnp.where(hidden[...].astype(F32) > 0, total[...], 0.0).astype(BF16)
    odd = lax.rem(lax.axis_index("slab"), 2)
    for q in range(lists.shape[3]):
        for ref, side in ((first, 1 - odd), (second, odd)):
            block = lists[0, 0, side, q]
            inside = jnp.minimum(block, blocks - 1)
            rows = plane_rows(3 * side, inside, blocks)
            for part, source in enumerate((hidden, grad_hidden)):
                value = source[rows, :]
                ref[q, :, part * channels : (part + 1) * channels] = jnp.where(
                    block < blocks, value, jnp.zeros_like(value)
                )
    fill_planes(
        planes,
        lambda x, b: features[0, b, x * ROWS : (x + 1) * ROWS, :],
        blocks,
        got_first,
        got_second,
        pl.ds(0, channels),
    )
    gather_shifts(shifted, planes, table, shift, blocks, slots)
    emit_gradient(
        lambda offset: over_voxels(taps_of(shifted, offset, blocks), grad_hidden[...]),
        grad,
        portions,
        outs,
        packed,
    )


def second_kernel(
    part, flipped, table, counts, source, got_first, got_second, shift, weight, rows, out, *rest
):
    planes, shifted, held, total, sem = rest
    blocks, channels = rows.shape[1], rows.shape[3]
    slots = planes.shape[0] // (4 * ROWS)
    fetch = pltpu.make_async_copy(weight, held, sem)
    fetch.start()
    fill_planes(
        planes,
        lambda x, b: source[plane_rows(x, b, blocks), :],
        blocks,
        got_first,
        got_second,
        pl.ds(part * channels, channels),
    )
    gather_shifts(shifted, planes, table, shift, blocks, slots)
    fetch.wait()
    convolve(total, shifted, held, blocks, flipped)
    for b in range(blocks):
        present = (b < counts[0, 0]).astype(F32)
        for x in range(4):
            at = slice(x * ROWS, (x + 1) * ROWS)
            added = rows[0, b, at, :].astype(F32)
            term = total[plane_rows(x, b, blocks), :]
            value = (added + term) * present if flipped else added * present + term
            out[0, b, at, :] = value.astype(BF16)


def unpack_kernel(factor, sizes, *refs):
    ins, outs = refs[:-2], refs[-2:]
    core = lax.rem(lax.axis_index("dp"), 2)
    at = 0
    for out, portions in zip(outs, sizes):
        half = out.shape[0] // 2
        for first, last in portions:
            value = (ins[at][...].astype(F32) + ins[at + 1][...].astype(F32)) * factor
            at += 2
            turned = pltpu.roll(value, 64, 1)
            even = core == 0
            out[first:last, :] = jnp.where(even, value, turned)[:, :64]
            out[half + first : half + last, :] = jnp.where(even, turned, value)[:, :64]


def call(kernel, outs, ins, places, scratch=()):
    spaces = {"s": pltpu.SMEM, "v": pltpu.VMEM, "h": pl.ANY}
    return pl.pallas_call(
        kernel,
        out_shape=outs,
        in_specs=[pl.BlockSpec(memory_space=spaces[place]) for place in places],
        out_specs=[pl.BlockSpec(memory_space=pltpu.VMEM) for _ in outs],
        scratch_shapes=list(scratch),
        compiler_params=pltpu.CompilerParams(vmem_limit_bytes=VMEM_LIMIT),
    )(*ins)


def add_and_split(keep, got):
    total = keep + got
    half = total.shape[0] // 2
    return total[:half], total[half:]


def reduce_packed(keep, send, order):
    got = swap(send, "core")
    for name in order:
        keep, send = add_and_split(keep, got)
        got = swap(send, name)
    return keep[0], got[0]


def per_device(
    features, cotangent, neighbour_table, send_lists, block_counts, weight_one, weight_two
):
    blocks, channels = features.shape[1], features.shape[3]
    dp_size, slab_size = lax.axis_size("dp"), lax.axis_size("slab")
    edge = send_lists.shape[3]
    taps_in = weight_one.shape[0]
    factor = 1.0 / math.sqrt(dp_size * slab_size * blocks * 64)
    voxels = blocks * 64
    slots = blocks + 2 * edge + 1
    packed = slab_size if (dp_size, slab_size, channels) == (4, 8, 256) else 0
    shift = jnp.asarray(shift_matrix(), BF16)

    def array(*shape, dtype=BF16):
        return jax.ShapeDtypeStruct(shape, dtype)

    def share_shapes(portions):
        if not packed:
            return [array(taps_in, channels, dtype=F32)]
        return [array(16, last - first, 128) for first, last, _ in portions for _ in range(2)]

    edges = array(edge, ROWS, 2 * channels)
    base = [
        pltpu.VMEM((slots * 64, channels), BF16),
        pltpu.VMEM((9 * 6 * blocks * ROWS, channels), BF16),
        pltpu.VMEM((taps_in, channels), BF16),
        pltpu.VMEM((voxels, channels), F32),
    ]
    full = pltpu.VMEM((taps_in, channels) if packed else (8, channels), F32)
    sem = pltpu.SemaphoreType.DMA

    first, second = call(
        pack_kernel,
        [edges, edges],
        (send_lists, features, cotangent),
        "shh",
        [pltpu.VMEM((2, edge, ROWS, 2 * channels), BF16), sem((2, edge, 2))],
    )
    got_first, got_second = swap_halos(first, second)
    hidden, *shares_two = call(
        functools.partial(forward_kernel, packed, PORTIONS["two"]),
        [array(voxels, channels)] + share_shapes(PORTIONS["two"]),
        (neighbour_table, features, cotangent, got_first, got_second, shift, weight_one),
        "svvvvvh",
        base + [full, sem],
    )
    grad_hidden, first, second, *shares_one = call(
        functools.partial(backward_kernel, packed, PORTIONS["one"]),
        [array(voxels, channels), edges, edges] + share_shapes(PORTIONS["one"]),
        (
            neighbour_table,
            send_lists,
            features,
            cotangent,
            got_first,
            got_second,
            shift,
            weight_two,
            hidden,
        ),
        "ssvvvvvhv",
        base + [full, sem],
    )
    got_first, got_second = swap_halos(first, second)
    (output,) = call(
        functools.partial(second_kernel, 0, False),
        [array(*features.shape)],
        (
            neighbour_table,
            block_counts,
            hidden,
            got_first,
            got_second,
            shift,
            weight_two,
            features,
        ),
        "ssvvvvhv",
        base + [sem],
    )
    (grad_features,) = call(
        functools.partial(second_kernel, 1, True),
        [array(*features.shape)],
        (
            neighbour_table,
            block_counts,
            grad_hidden,
            got_first,
            got_second,
            shift,
            weight_one,
            cotangent,
        ),
        "ssvvvvhv",
        base + [sem],
    )
    if packed:
        terms, sizes = [], []
        for shares, portions in ((shares_one, PORTIONS["one"]), (shares_two, PORTIONS["two"])):
            sizes.append([(start, last) for start, last, _ in portions])
            for keep, send, (_, _, order) in zip(shares[0::2], shares[1::2], portions):
                terms += reduce_packed(keep, send, order)
        out = array(taps_in // slab_size, channels // dp_size, dtype=F32)
        grad_one, grad_two = call(
            functools.partial(unpack_kernel, factor, sizes), [out, out], terms, "v" * len(terms)
        )
    else:
        grad_one, grad_two = (
            lax.psum_scatter(
                lax.psum_scatter(share, "slab", scatter_dimension=0, tiled=True),
                "dp",
                scatter_dimension=1,
                tiled=True,
            )
            * factor
            for (share,) in (shares_one, shares_two)
        )
    return (output, grad_features, grad_one, grad_two)


def solution(mesh):
    in_specs = (
        P("dp", "slab", None, None),
        P("dp", "slab", None, None),
        P("dp", "slab", None),
        P("dp", "slab", None, None),
        P("dp", "slab"),
        P(),
        P(),
    )
    out_specs = (
        P("dp", "slab", None, None),
        P("dp", "slab", None, None),
        P("slab", "dp"),
        P("slab", "dp"),
    )
    return jax.shard_map(
        per_device, mesh=mesh, in_specs=in_specs, out_specs=out_specs, check_vma=False
    )
```

```python
import functools
import math

import jax
import jax.numpy as jnp
from jax import lax
from jax.experimental import pallas as pl
from jax.experimental.pallas import tpu as pltpu
from jax.sharding import PartitionSpec as P

F32 = jnp.float32
BF16 = jnp.bfloat16
TAPS = 27
ROWS = 16
MIB = 2**20
SECOND_COST = 1
INNER_LIMIT = 44
FORWARD_LIMIT = 14
UNROLL = 5

ORDERS_ONE = (
    (0, 288, ("x", "y", "z1")),
    (288, 432, ("y", "x", "z1")),
)
ORDERS_TWO = (
    (0, 256, ("z1", "y", "x")),
    (256, 432, ("y", "z1", "x")),
)
LAST = "z2"


def shift_matrix():
    shape = (8 * ROWS, 9 * ROWS)
    row = lax.broadcasted_iota(jnp.int32, shape, 0)
    column = lax.broadcasted_iota(jnp.int32, shape, 1)
    shift = row >> 4
    shift = jnp.where(shift >= 4, shift + 1, shift)
    across = jnp.where(shift >= 6, 2, jnp.where(shift >= 3, 1, 0))
    y = ((row >> 2) & 3) + across + 3
    z = (row & 3) + (shift - 3 * across) + 3
    plane = 3 * (y >> 2) + (z >> 2)
    source = 16 * plane + 4 * (y & 3) + (z & 3)
    return jnp.where(column == source, 1.0, 0.0).astype(BF16)


def bit_of(name, dp_index, slab_index):
    if name == "y":
        return dp_index // 2
    if name == "x":
        return slab_index % 2
    if name == "z1":
        return slab_index // 2 % 2
    return slab_index // 4


def pair_perm(name, dp_size, slab_size):
    dp_flip = {"core": 1, "y": 2}.get(name, 0)
    slab_flip = {"x": 1, "z1": 2, "z2": 4}.get(name, 0)
    return [
        (d * slab_size + s, (d ^ dp_flip) * slab_size + (s ^ slab_flip))
        for d in range(dp_size)
        for s in range(slab_size)
    ]


def swap(array, name):
    dp_size, slab_size = lax.axis_size("dp"), lax.axis_size("slab")
    return lax.ppermute(array, ("dp", "slab"), pair_perm(name, dp_size, slab_size))


def swap_halos(first, second):
    count = lax.axis_size("slab")
    even = [(s, s ^ 1) for s in range(count) if s ^ 1 < count]
    odd = [(s, s + 1 if s % 2 else s - 1) for s in range(1, count) if s % 2 == 0 or s + 1 < count]
    return lax.ppermute(first, "slab", even), lax.ppermute(second, "slab", odd)


def pack_kernel(lists, features, cotangent, first, second, shift, planes, more, sems):
    blocks, channels = features.shape[1], features.shape[3]
    copies = start_planes(planes, features, blocks, sems.at[0])
    copies += start_planes(more, cotangent, blocks, sems.at[1])
    shift[...] = shift_matrix()
    for field in (planes, more):
        field[:, blocks:] = jnp.zeros_like(field[:, blocks:])
    for copy in copies:
        copy.wait()
    pack_edges(lists, (planes, more), blocks, first, second)


def pack_edges(lists, fields, blocks, first, second):
    channels = fields[0].shape[3]
    odd = lax.rem(lax.axis_index("slab"), 2)
    for q in range(lists.shape[3]):
        for ref, side in ((first, 1 - odd), (second, odd)):
            block = lists[0, 0, side, q]
            inside = jnp.minimum(block, blocks - 1)
            for part, source in enumerate(fields):
                value = source[3 * side, inside]
                ref[q, :, part * channels : (part + 1) * channels] = jnp.where(
                    block < blocks, value, jnp.zeros_like(value)
                )


def start_planes(planes, source, blocks, sem):
    copies = []
    for x in range(4):
        if source.shape[2] != ROWS:
            piece = source.at[0, :, pl.ds(x * ROWS, ROWS), :]
        else:
            piece = source.at[x]
        copies.append(pltpu.make_async_copy(piece, planes.at[x, pl.ds(0, blocks)], sem.at[x]))
        copies[-1].start()
    return copies


def fill_edges(planes, blocks, got_first, got_second, lanes, places):
    edge = got_first.shape[0]
    planes[:, blocks:] = jnp.zeros_like(planes[:, blocks:])
    is_odd = lax.rem(lax.axis_index("slab"), 2) == 1
    for q in range(edge):
        one, two = got_first[q, :, lanes], got_second[q, :, lanes]
        planes[places[0], blocks + q] = jnp.where(is_odd, one, two)
        planes[places[1], blocks + edge + q] = jnp.where(is_odd, two, one)


def gather_shifts(shifted, planes, table, shift, blocks, wanted):
    matrix = shift[...]

    def one_block(b, carry):
        for place, (at, slab) in enumerate(wanted):
            near_x = 0 if at == 0 else 2 if at == 5 else 1
            around = [planes[slab, table[0, b, 9 * near_x + n]] for n in range(9)]
            moved = jnp.dot(
                matrix, jnp.concatenate(around, axis=0), preferred_element_type=F32
            ).astype(BF16)
            pieces = [moved[n * ROWS : (n + 1) * ROWS] for n in range(8)]
            pieces.insert(4, around[4])
            for n, piece in enumerate(pieces):
                start = place * blocks * ROWS + b * ROWS
                shifted[n, pl.ds(pl.multiple_of(start, ROWS), ROWS), :] = piece
        return carry

    lax.fori_loop(0, blocks, one_block, 0, unroll=UNROLL)


INNER = ((1, 0), (2, 1), (3, 2), (4, 3))
OUTER = ((0, 0), (5, 1))


def inner_taps(inner, offset):
    step = inner.shape[1] // 4
    along_x, along_yz = offset // 9, offset % 9
    if along_x == 0:
        return inner[along_yz, : 3 * step, :], step
    return inner[along_yz, (along_x - 1) * step :, :], 0


def taps_of(inner, outer, offset):
    step = inner.shape[1] // 4
    along_x, along_yz = offset // 9, offset % 9
    own, _ = inner_taps(inner, offset)
    if along_x == 0:
        return jnp.concatenate([outer[along_yz, :step, :], own], axis=0)
    if along_x == 2:
        return jnp.concatenate([own, outer[along_yz, step:, :]], axis=0)
    return own


def tap_weight(weight, offset, flipped):
    channels = weight.shape[1]
    row = (TAPS - 1 - offset if flipped else offset) * channels
    return weight[row : row + channels, :]


def times(left, right, flipped):
    return lax.dot_general(
        left, right, (((1,), (1 if flipped else 0,)), ((), ())), preferred_element_type=F32
    )


def convolve(total, inner, outer, weight, flipped):
    order = list(range(9, 18)) + list(range(9)) + list(range(18, 27))
    for at, offset in enumerate(order):
        if outer is None:
            taps, first = inner_taps(inner, offset)
        else:
            taps, first = taps_of(inner, outer, offset), 0
        term = times(taps, tap_weight(weight, offset, flipped), flipped)
        if at == 0:
            total[...] = term
        else:
            total[first : first + term.shape[0], :] += term


def emit_share(grad, dest, portions, outs, tile_rows, slab_size):
    half = tile_rows // 2
    dp_index, slab_index = lax.axis_index("dp"), lax.axis_index("slab")
    core = lax.rem(dp_index, 2)
    lane = lax.broadcasted_iota(jnp.int32, (half, 128), 1)
    low = (lane < 64) == (core == 0)
    for y in range(2):
        upper = grad[dest * tile_rows : dest * tile_rows + half, y * 128 : (y + 1) * 128]
        lower = grad[dest * tile_rows + half : (dest + 1) * tile_rows, y * 128 : (y + 1) * 128]
        lower = pltpu.roll(lower, 64, 1)
        keep = jnp.where(low, upper, lower).astype(BF16)
        send = jnp.where(low, lower, upper).astype(BF16)
        keep_ref, send_ref = outs
        for first, last, order in portions:
            index = 0
            for name in order + (LAST,):
                bit = bit_of(name, dp_index, slab_index)
                mine = y if name == "y" else bit_of(name, 0, dest)
                index = index * 2 + (bit ^ mine)
            keep_ref[index, first:last] = keep[first:last]
            send_ref[index, first:last] = send[first:last]


def emit_gradient(product, grad, portions, outs, packed):
    channels = grad.shape[1]
    if not packed:
        for offset in range(TAPS):
            outs[0][offset * channels : (offset + 1) * channels, :] = product(offset)
        return
    slab_size = packed
    tile_rows = TAPS * channels // slab_size
    done = 0
    for offset in range(TAPS):
        grad[offset * channels : (offset + 1) * channels, :] = product(offset)
        while done < slab_size and (done + 1) * tile_rows <= (offset + 1) * channels:
            emit_share(grad, done, portions, outs, tile_rows, slab_size)
            done += 1


def over_voxels(left, right):
    return lax.dot_general(left, right, (((0,), (0,)), ((), ())), preferred_element_type=F32)


def inner_kernel(table, planes, more, shift, weight, inner, other, before, held, sem):
    blocks = before.shape[0] // 64
    fetch = pltpu.make_async_copy(weight, held, sem)
    fetch.start()
    gather_shifts(inner, planes, table, shift, blocks, INNER)
    gather_shifts(other, more, table, shift, blocks, INNER)
    fetch.wait()
    convolve(before, inner, None, held, False)


def forward_kernel(
    packed,
    portions,
    table,
    source,
    source_other,
    got_first,
    got_second,
    shift,
    weight,
    inner,
    other,
    before,
    hidden,
    outer,
    outer_other,
    *rest,
):
    *outs, planes, grad, held, sem = rest
    fetch = pltpu.make_async_copy(weight, held, sem)
    fetch.start()
    blocks, channels = hidden.shape[1], hidden.shape[3]
    step = blocks * ROWS
    for part, (field, target) in enumerate(((source, outer), (source_other, outer_other))):
        planes[0] = field[3]
        planes[1] = field[0]
        fill_edges(
            planes, blocks, got_first, got_second, pl.ds(part * channels, channels), (0, 1)
        )
        gather_shifts(target, planes, table, shift, blocks, OUTER)
    fetch.wait()
    for x in range(4):
        value = before[x * step : (x + 1) * step, :]
        if x in (0, 3):
            for n in range(9):
                taps = outer[n, :step, :] if x == 0 else outer[n, step:, :]
                value += times(taps, tap_weight(held, n if x == 0 else 18 + n, False), False)
        hidden[x] = jnp.maximum(value, 0.0).astype(BF16).reshape(hidden.shape[1:])
    left = hidden[...].reshape(4 * step, channels)
    emit_gradient(
        lambda offset: over_voxels(left, taps_of(other, outer_other, TAPS - 1 - offset)),
        grad,
        portions,
        outs,
        packed,
    )


def middle_kernel(
    lists, inner, outer, weight, hidden, grad_hidden, first, second, total
):
    blocks, channels = hidden.shape[1], hidden.shape[3]
    convolve(total, inner, outer, weight, True)
    kept = jnp.where(hidden[...].reshape(total.shape).astype(F32) > 0, total[...], 0.0)
    grad_hidden[...] = kept.astype(BF16).reshape(grad_hidden.shape)
    pack_edges(lists, (hidden, grad_hidden), blocks, first, second)


def backward_kernel(packed, portions, inner, outer, grad_hidden, *rest):
    *outs, grad = rest
    blocks, channels = grad_hidden.shape[1], grad_hidden.shape[3]
    right = grad_hidden[...].reshape(blocks * 64, channels)
    emit_gradient(
        lambda offset: over_voxels(taps_of(inner, outer, offset), right),
        grad,
        portions,
        outs,
        packed,
    )


def second_kernel(
    part, flipped, tokens, table, counts, source, got_first, got_second, shift, weight, rows, *rest
):
    out, planes, own, inner, outer, total, sem = rest[tokens:]
    blocks, channels = rows.shape[1], rows.shape[3]
    later = pltpu.make_async_copy(rows.at[0], own, sem)
    later.start()
    planes[:, :blocks] = source[...]
    fill_edges(
        planes, blocks, got_first, got_second, pl.ds(part * channels, channels), (3, 0)
    )
    gather_shifts(inner, planes, table, shift, blocks, INNER)
    gather_shifts(outer, planes, table, shift, blocks, ((0, 3), (5, 0)))
    convolve(total, inner, outer, weight, flipped)
    later.wait()
    for b in range(blocks):
        present = (b < counts[0, 0]).astype(F32)
        for x in range(4):
            at = slice(x * ROWS, (x + 1) * ROWS)
            added = own[b, at, :].astype(F32)
            start = (x * blocks + b) * ROWS
            term = total[start : start + ROWS, :]
            value = (added + term) * present if flipped else added * present + term
            out[0, b, at, :] = value.astype(BF16)


def unpack_kernel(factor, *refs):
    ins, outs = refs[:-2], refs[-2:]
    core = lax.rem(lax.axis_index("dp"), 2)
    for keep, got, out in zip(ins[0::2], ins[1::2], outs):
        columns = out.shape[0]
        whole = (keep[...].astype(F32) + got[...].astype(F32)) * factor
        whole = jnp.where(core == 0, whole, pltpu.roll(whole, columns, 1)).T
        out[...] = jnp.concatenate([whole[:columns], whole[columns:]], axis=1)


def call(kernel, outs, ins, places, scratch=(), limit=24, flops=0):
    spaces = {"s": pltpu.SMEM, "v": pltpu.VMEM, "a": pl.ANY, "h": pltpu.HBM}
    return pl.pallas_call(
        kernel,
        out_shape=outs,
        in_specs=[pl.BlockSpec(memory_space=spaces[place]) for place in places],
        out_specs=[pl.BlockSpec(memory_space=pltpu.VMEM) for _ in outs],
        scratch_shapes=list(scratch),
        compiler_params=pltpu.CompilerParams(vmem_limit_bytes=limit * MIB),
        cost_estimate=pl.CostEstimate(flops=flops, bytes_accessed=0, transcendentals=0),
    )(*ins)


def halves(array):
    half = array.shape[0] // 2
    return array[:half], array[half:]


def add_terms(parts):
    pairs = [halves(keep + got) for keep, got in parts]
    return [keep for keep, _ in pairs], [send for _, send in pairs]


def swaps(keeps, sends, names):
    return [[keep, swap(send, name)] for keep, send, name in zip(keeps, sends, names)]


def join(parts):
    return [[jnp.concatenate([part[i] for part in parts], axis=1) for i in range(2)]]


def fence(parts, others):
    keeps, others = lax.optimization_barrier(([keep for keep, _ in parts], others))
    return [[keep, got] for keep, (_, got) in zip(keeps, parts)], others


def reduce_packed(shares_one, shares_two, edges, finish):
    two, one = (
        [[keep[:, first:last], got[:, first:last]] for first, last, _ in orders]
        for keep, got, orders in (
            (shares_two[0], swap(shares_two[1], "core"), ORDERS_TWO),
            (shares_one[0], swap(shares_one[1], "core"), ORDERS_ONE),
        )
    )
    names_two = list(zip(*(order for _, _, order in ORDERS_TWO)))
    names_one = list(zip(*(order for _, _, order in ORDERS_ONE)))
    results = []
    halos = swap_halos(*edges)
    for step in range(2):
        keeps, sends = add_terms(two)
        one, sends = fence(one, sends)
        two = swaps(keeps, sends, names_two[step])
        keeps, sends = add_terms(one)
        one = swaps(keeps, sends, names_one[step])
        results.append(finish(step, sends, halos))
        two, results[-1] = fence(two, results[-1])
    keeps, sends = add_terms(join(two))
    one, sends = fence(one, sends)
    two = swaps(keeps, sends, names_two[2][:1])
    keeps, sends = add_terms(join(one))
    two, sends = fence(two, sends)
    one = swaps(keeps, sends, names_one[2][:1])
    keeps, sends = add_terms(two)
    one, sends = fence(one, sends)
    two = swaps(keeps, sends, [LAST])
    keeps, sends = add_terms(one)
    one = swaps(keeps, sends, [LAST])
    return [term[0] for term in one[0] + two[0]], results


def per_device(
    features, cotangent, neighbour_table, send_lists, block_counts, weight_one, weight_two
):
    blocks, channels = features.shape[1], features.shape[3]
    dp_size, slab_size = lax.axis_size("dp"), lax.axis_size("slab")
    edge = send_lists.shape[3]
    taps_in = weight_one.shape[0]
    factor = 1.0 / math.sqrt(dp_size * slab_size * blocks * 64)
    voxels = blocks * 64
    slots = blocks + 2 * edge + 1
    packed = slab_size if (dp_size, slab_size, channels) == (4, 8, 256) else 0

    def array(*shape, dtype=BF16):
        return jax.ShapeDtypeStruct(shape, dtype)

    if packed:
        shares = [array(16, taps_in // slab_size // 2, 128)] * 2
    else:
        shares = [array(taps_in, channels, dtype=F32)]
    edges = array(edge, ROWS, 2 * channels)
    planes = pltpu.VMEM((4, slots, ROWS, channels), BF16)
    ends = pltpu.VMEM((2, slots, ROWS, channels), BF16)
    inner_shape = array(9, 4 * blocks * ROWS, channels)
    outer_shape = array(9, 2 * blocks * ROWS, channels)
    total = array(voxels, channels, dtype=F32)
    full = pltpu.VMEM((taps_in, channels) if packed else (8, channels), F32)
    sem = pltpu.SemaphoreType.DMA
    field = array(4, blocks, ROWS, channels)
    held = array(taps_in, channels)

    def scratch(shape):
        return pltpu.VMEM(shape.shape, shape.dtype)

    product = 2 * voxels * taps_in * channels
    around = array(4, slots, ROWS, channels)
    first, second, shift, source, source_other = call(
        pack_kernel,
        [edges, edges, array(8 * ROWS, 9 * ROWS), around, around],
        (send_lists, features, cotangent),
        "shh",
        [sem((2, 4))],
        limit=6,
    )
    got_first, got_second = swap_halos(first, second)
    inner, inner_other, before = call(
        inner_kernel,
        [inner_shape, inner_shape, total],
        (neighbour_table, source, source_other, shift, weight_one),
        "svvvh",
        [scratch(held), sem],
        limit=INNER_LIMIT,
        flops=2 * product,
    )
    hidden, outer, outer_other, *shares_two = call(
        functools.partial(forward_kernel, packed, ORDERS_TWO),
        [field, outer_shape, outer_shape] + shares,
        (
            neighbour_table,
            source,
            source_other,
            got_first,
            got_second,
            shift,
            weight_one,
            inner,
            inner_other,
            before,
        ),
        "svvvvvhvvv",
        [ends, full, scratch(held), sem],
        limit=FORWARD_LIMIT,
        flops=2 * product,
    )
    grad_hidden, first, second = call(
        middle_kernel,
        [field, edges, edges],
        (send_lists, inner_other, outer_other, weight_two, hidden),
        "svvvv",
        [scratch(total)],
        limit=4,
        flops=product,
    )
    shares_one = call(
        functools.partial(backward_kernel, packed, ORDERS_ONE),
        shares,
        (inner, outer, grad_hidden),
        "vvv",
        [full],
        limit=10,
        flops=product,
    )
    seconds = (
        (hidden, weight_two, features),
        (grad_hidden, weight_one, cotangent),
    )

    def finish(part, tokens, halos):
        got_first, got_second = halos
        source, weight, rows = seconds[part]
        (out,) = call(
            functools.partial(second_kernel, part, part == 1, len(tokens)),
            [array(*features.shape)],
            (
                neighbour_table,
                block_counts,
                source,
                got_first,
                got_second,
                shift,
                weight,
                rows,
                *tokens,
            ),
            "ssvvvvva" + "a" * len(tokens),
            [
                planes,
                pltpu.VMEM((blocks, 64, channels), BF16),
                scratch(inner_shape),
                scratch(outer_shape),
                scratch(total),
                sem,
            ],
            limit=10,
            flops=SECOND_COST * product,
        )
        return out

    if packed:
        terms, (output, grad_features) = reduce_packed(
            shares_one, shares_two, (first, second), finish
        )
        out = array(channels // dp_size, taps_in // slab_size, dtype=F32)
        grad_one, grad_two = (
            turned.T
            for turned in call(
                functools.partial(unpack_kernel, factor), [out, out], terms, "v" * len(terms)
            )
        )
    else:
        halos = swap_halos(first, second)
        output, grad_features = finish(0, [], halos), finish(1, [], halos)
        grad_one, grad_two = (
            lax.psum_scatter(
                lax.psum_scatter(share, "slab", scatter_dimension=0, tiled=True),
                "dp",
                scatter_dimension=1,
                tiled=True,
            )
            * factor
            for (share,) in (shares_one, shares_two)
        )
    return (output, grad_features, grad_one, grad_two)


def solution(mesh):
    in_specs = (
        P("dp", "slab", None, None),
        P("dp", "slab", None, None),
        P("dp", "slab", None),
        P("dp", "slab", None, None),
        P("dp", "slab"),
        P(),
        P(),
    )
    out_specs = (
        P("dp", "slab", None, None),
        P("dp", "slab", None, None),
        P("slab", "dp"),
        P("slab", "dp"),
    )
    return jax.shard_map(
        per_device, mesh=mesh, in_specs=in_specs, out_specs=out_specs, check_vma=False
    )
```

```python
import functools
import math

import jax
import jax.numpy as jnp
from jax import lax
from jax.experimental import pallas as pl
from jax.experimental.pallas import tpu as pltpu
from jax.sharding import PartitionSpec as P

F32 = jnp.float32
BF16 = jnp.bfloat16
TAPS = 27
ROWS = 16
MIB = 2**20
SECOND_COST = 1
INNER_LIMIT = 42
FORWARD_LIMIT = 14
UNROLL = 5

ORDERS_ONE = (
    (0, 288, ("z1", "y", "x")),
    (288, 432, ("y", "z1", "x")),
)
ORDERS_TWO = (
    (0, 256, ("x", "y", "z1")),
    (256, 432, ("y", "x", "z1")),
)
LAST = "z2"


def shift_matrix():
    shape = (16 * ROWS, 12 * ROWS)
    row = lax.broadcasted_iota(jnp.int32, shape, 0)
    column = lax.broadcasted_iota(jnp.int32, shape, 1)
    shift = (row >> 4) & 7
    shift = jnp.where(shift >= 4, shift + 1, shift)
    across = jnp.where(shift >= 6, 2, jnp.where(shift >= 3, 1, 0))
    y = ((row >> 2) & 3) + across + 3
    z = (row & 3) + (shift - 3 * across) + 3
    own = jnp.where((y >> 2) == 1, 16, 0)
    source = 32 * (z >> 2) + own + 4 * (y & 3) + (z & 3)
    return jnp.where(column == source + 96 * (row >> 7), 1.0, 0.0).astype(BF16)


def bit_of(name, dp_index, slab_index):
    if name == "y":
        return dp_index // 2
    if name == "x":
        return slab_index % 2
    if name == "z1":
        return slab_index // 2 % 2
    return slab_index // 4


def pair_perm(name, dp_size, slab_size):
    dp_flip = {"core": 1, "y": 2}.get(name, 0)
    slab_flip = {"x": 1, "z1": 2, "z2": 4}.get(name, 0)
    return [
        (d * slab_size + s, (d ^ dp_flip) * slab_size + (s ^ slab_flip))
        for d in range(dp_size)
        for s in range(slab_size)
    ]


def swap(array, name):
    dp_size, slab_size = lax.axis_size("dp"), lax.axis_size("slab")
    return lax.ppermute(array, ("dp", "slab"), pair_perm(name, dp_size, slab_size))


def swap_halos(first, second):
    count = lax.axis_size("slab")
    even = [(s, s ^ 1) for s in range(count) if s ^ 1 < count]
    odd = [(s, s + 1 if s % 2 else s - 1) for s in range(1, count) if s % 2 == 0 or s + 1 < count]
    return lax.ppermute(first, "slab", even), lax.ppermute(second, "slab", odd)


def pack_kernel(lists, fields, first, second, shift, planes, more, sems):
    blocks = fields.shape[1]
    copies = start_planes(planes, fields.at[0:1], blocks, sems.at[0])
    copies += start_planes(more, fields.at[1:2], blocks, sems.at[1])
    shift[...] = shift_matrix()
    for field in (planes, more):
        field[:, blocks:] = jnp.zeros_like(field[:, blocks:])
    for copy in copies:
        copy.wait()
    pack_edges(lists, (planes, more), blocks, first, second)


def pack_edges(lists, fields, blocks, first, second):
    channels = fields[0].shape[3]
    odd = lax.rem(lax.axis_index("slab"), 2)
    for q in range(lists.shape[3]):
        for ref, side in ((first, 1 - odd), (second, odd)):
            block = lists[0, 0, side, q]
            inside = jnp.minimum(block, blocks - 1)
            for part, source in enumerate(fields):
                value = source[3 * side, inside]
                ref[q, :, part * channels : (part + 1) * channels] = jnp.where(
                    block < blocks, value, jnp.zeros_like(value)
                )


def start_planes(planes, source, blocks, sem):
    copies = []
    for x in range(4):
        if source.shape[2] != ROWS:
            piece = source.at[0, :, pl.ds(x * ROWS, ROWS), :]
        else:
            piece = source.at[x]
        copies.append(pltpu.make_async_copy(piece, planes.at[x, pl.ds(0, blocks)], sem.at[x]))
        copies[-1].start()
    return copies


def fill_edges(planes, blocks, got_first, got_second, lanes, places):
    edge = got_first.shape[0]
    planes[:, blocks:] = jnp.zeros_like(planes[:, blocks:])
    is_odd = lax.rem(lax.axis_index("slab"), 2) == 1
    for q in range(edge):
        one, two = got_first[q, :, lanes], got_second[q, :, lanes]
        planes[places[0], blocks + q] = jnp.where(is_odd, one, two)
        planes[places[1], blocks + edge + q] = jnp.where(is_odd, two, one)


def gather_shifts(shifted, planes, table, shift, blocks, wanted):
    matrix = shift[...]
    upper = lax.broadcasted_iota(jnp.int32, (ROWS, planes.shape[3]), 0) < 8

    def one_block(b, carry):
        for place in range(0, len(wanted), 2):
            stack, centres = [], []
            for at, slab in wanted[place : place + 2]:
                near_x = 0 if at == 0 else 2 if at == 5 else 1
                around = [planes[slab, table[b, 0, 9 * near_x + n]] for n in range(9)]
                for z in range(3):
                    stack += [jnp.where(upper, around[6 + z], around[z]), around[3 + z]]
                centres.append(around[4])
            moved = jnp.dot(
                matrix, jnp.concatenate(stack, axis=0), preferred_element_type=F32
            ).astype(BF16)
            for half in range(2):
                pieces = [
                    moved[(8 * half + n) * ROWS : (8 * half + n + 1) * ROWS] for n in range(8)
                ]
                pieces.insert(4, centres[half])
                for n, piece in enumerate(pieces):
                    start = (place + half) * blocks * ROWS + b * ROWS
                    shifted[n, pl.ds(pl.multiple_of(start, ROWS), ROWS), :] = piece
        return carry

    lax.fori_loop(0, blocks, one_block, 0, unroll=UNROLL)


INNER = ((1, 0), (2, 1), (3, 2), (4, 3))
OUTER = ((0, 0), (5, 1))


def inner_taps(inner, offset):
    step = inner.shape[1] // 4
    along_x, along_yz = offset // 9, offset % 9
    if along_x == 0:
        return inner[along_yz, : 3 * step, :], step
    return inner[along_yz, (along_x - 1) * step :, :], 0


def taps_of(inner, outer, offset):
    step = inner.shape[1] // 4
    along_x, along_yz = offset // 9, offset % 9
    own, _ = inner_taps(inner, offset)
    if along_x == 0:
        return jnp.concatenate([outer[along_yz, :step, :], own], axis=0)
    if along_x == 2:
        return jnp.concatenate([own, outer[along_yz, step:, :]], axis=0)
    return own


def tap_weight(weight, offset, flipped):
    channels = weight.shape[1]
    row = (TAPS - 1 - offset if flipped else offset) * channels
    return weight[row : row + channels, :]


def times(left, right, flipped):
    return lax.dot_general(
        left, right, (((1,), (1 if flipped else 0,)), ((), ())), preferred_element_type=F32
    )


def convolve(total, inner, outer, weight, flipped):
    order = list(range(9, 18)) + list(range(9)) + list(range(18, 27))
    for at, offset in enumerate(order):
        if outer is None:
            taps, first = inner_taps(inner, offset)
        else:
            taps, first = taps_of(inner, outer, offset), 0
        term = times(taps, tap_weight(weight, offset, flipped), flipped)
        if at == 0:
            total[...] = term
        else:
            total[first : first + term.shape[0], :] += term


def emit_share(grad, dest, portions, outs, tile_rows, slab_size):
    half = tile_rows // 2
    dp_index, slab_index = lax.axis_index("dp"), lax.axis_index("slab")
    core = lax.rem(dp_index, 2)
    lane = lax.broadcasted_iota(jnp.int32, (half, 128), 1)
    low = (lane < 64) == (core == 0)
    for y in range(2):
        upper = grad[dest * tile_rows : dest * tile_rows + half, y * 128 : (y + 1) * 128]
        lower = grad[dest * tile_rows + half : (dest + 1) * tile_rows, y * 128 : (y + 1) * 128]
        lower = pltpu.roll(lower, 64, 1)
        keep = jnp.where(low, upper, lower).astype(BF16)
        send = jnp.where(low, lower, upper).astype(BF16)
        keep_ref, send_ref = outs
        for first, last, order in portions:
            index = 0
            for name in order + (LAST,):
                bit = bit_of(name, dp_index, slab_index)
                mine = y if name == "y" else bit_of(name, 0, dest)
                index = index * 2 + (bit ^ mine)
            keep_ref[index, first:last] = keep[first:last]
            send_ref[index, first:last] = send[first:last]


def emit_gradient(product, grad, portions, outs, packed):
    channels = grad.shape[1]
    if not packed:
        for offset in range(TAPS):
            outs[0][offset * channels : (offset + 1) * channels, :] = product(offset)
        return
    slab_size = packed
    tile_rows = TAPS * channels // slab_size
    done = 0
    for offset in range(TAPS):
        grad[offset * channels : (offset + 1) * channels, :] = product(offset)
        while done < slab_size and (done + 1) * tile_rows <= (offset + 1) * channels:
            emit_share(grad, done, portions, outs, tile_rows, slab_size)
            done += 1


def over_voxels(left, right):
    return lax.dot_general(left, right, (((0,), (0,)), ((), ())), preferred_element_type=F32)


def inner_kernel(table, planes, more, shift, weight, inner, other, before, held, sem):
    blocks = before.shape[0] // 64
    third = weight.shape[0] // 3
    fetches = []
    for i in (1, 0, 2):
        rows = pl.ds(i * third, third)
        fetches.append(pltpu.make_async_copy(weight.at[rows], held.at[rows], sem.at[i]))
        fetches[-1].start()
    gather_shifts(inner, planes, table, shift, blocks, INNER)
    gather_shifts(other, more, table, shift, blocks, INNER)
    for fetch in fetches:
        fetch.wait()
    convolve(before, inner, None, held, False)


def forward_kernel(
    packed,
    portions,
    table,
    source,
    source_other,
    got_first,
    got_second,
    shift,
    weight,
    inner,
    other,
    before,
    hidden,
    outer,
    outer_other,
    *rest,
):
    *outs, planes, grad = rest
    blocks, channels = hidden.shape[1], hidden.shape[3]
    step = blocks * ROWS
    for part, (field, target) in enumerate(((source, outer), (source_other, outer_other))):
        planes[0] = field[3]
        planes[1] = field[0]
        fill_edges(
            planes, blocks, got_first, got_second, pl.ds(part * channels, channels), (0, 1)
        )
        gather_shifts(target, planes, table, shift, blocks, OUTER)
    for x in range(4):
        value = before[x * step : (x + 1) * step, :]
        if x in (0, 3):
            for n in range(9):
                taps = outer[n, :step, :] if x == 0 else outer[n, step:, :]
                value += times(taps, tap_weight(weight, n if x == 0 else 18 + n, False), False)
        hidden[x] = jnp.maximum(value, 0.0).astype(BF16).reshape(hidden.shape[1:])
    left = hidden[...].reshape(4 * step, channels)
    emit_gradient(
        lambda offset: over_voxels(left, taps_of(other, outer_other, TAPS - 1 - offset)),
        grad,
        portions,
        outs,
        packed,
    )


def middle_kernel(
    lists, inner, outer, weight, hidden, grad_hidden, first, second, total
):
    blocks, channels = hidden.shape[1], hidden.shape[3]
    convolve(total, inner, outer, weight, True)
    kept = jnp.where(hidden[...].reshape(total.shape).astype(F32) > 0, total[...], 0.0)
    grad_hidden[...] = kept.astype(BF16).reshape(grad_hidden.shape)
    pack_edges(lists, (hidden, grad_hidden), blocks, first, second)


def backward_kernel(packed, portions, inner, outer, grad_hidden, *rest):
    *outs, grad = rest
    blocks, channels = grad_hidden.shape[1], grad_hidden.shape[3]
    right = grad_hidden[...].reshape(blocks * 64, channels)
    emit_gradient(
        lambda offset: over_voxels(taps_of(inner, outer, offset), right),
        grad,
        portions,
        outs,
        packed,
    )


def second_kernel(
    part, flipped, tokens, table, counts, source, got_first, got_second, shift, weight, rows, *rest
):
    out, planes, own, inner, outer, total, sem = rest[tokens:]
    blocks, channels = rows.shape[1], rows.shape[3]
    later = pltpu.make_async_copy(rows.at[0], own, sem)
    later.start()
    planes[:, :blocks] = source[...]
    fill_edges(
        planes, blocks, got_first, got_second, pl.ds(part * channels, channels), (3, 0)
    )
    gather_shifts(inner, planes, table, shift, blocks, INNER)
    gather_shifts(outer, planes, table, shift, blocks, ((0, 3), (5, 0)))
    convolve(total, inner, outer, weight, flipped)
    later.wait()
    for b in range(blocks):
        present = (b < counts[0, 0]).astype(F32)
        for x in range(4):
            at = slice(x * ROWS, (x + 1) * ROWS)
            added = own[b, at, :].astype(F32)
            start = (x * blocks + b) * ROWS
            term = total[start : start + ROWS, :]
            value = (added + term) * present if flipped else added * present + term
            out[0, b, at, :] = value.astype(BF16)


def unpack_kernel(factor, keep, got, out):
    core = lax.rem(lax.axis_index("dp"), 2)
    columns = out.shape[0]
    whole = (keep[...].astype(F32) + got[...].astype(F32)) * factor
    whole = jnp.where(core == 0, whole, pltpu.roll(whole, columns, 1)).T
    out[...] = jnp.concatenate([whole[:columns], whole[columns:]], axis=1)


def call(kernel, outs, ins, places, scratch=(), limit=24, flops=0):
    spaces = {"s": pltpu.SMEM, "v": pltpu.VMEM, "a": pl.ANY, "h": pltpu.HBM}
    return pl.pallas_call(
        kernel,
        out_shape=outs,
        in_specs=[pl.BlockSpec(memory_space=spaces[place]) for place in places],
        out_specs=[pl.BlockSpec(memory_space=pltpu.VMEM) for _ in outs],
        scratch_shapes=list(scratch),
        compiler_params=pltpu.CompilerParams(vmem_limit_bytes=limit * MIB),
        cost_estimate=pl.CostEstimate(flops=flops, bytes_accessed=0, transcendentals=0),
    )(*ins)


def halves(array):
    half = array.shape[0] // 2
    return array[:half], array[half:]


def add_terms(parts):
    pairs = [halves(keep + got) for keep, got in parts]
    return [keep for keep, _ in pairs], [send for _, send in pairs]


def swaps(keeps, sends, names):
    return [[keep, swap(send, name)] for keep, send, name in zip(keeps, sends, names)]


def join(parts):
    return [[jnp.concatenate([part[i] for part in parts], axis=1) for i in range(2)]]


def fence(parts, others):
    keeps, others = lax.optimization_barrier(([keep for keep, _ in parts], others))
    return [[keep, got] for keep, (_, got) in zip(keeps, parts)], others


def reduce_packed(shares_one, shares_two, edges, finish):
    two, one = (
        [[keep[:, first:last], got[:, first:last]] for first, last, _ in orders]
        for keep, got, orders in (
            (shares_two[0], swap(shares_two[1], "core"), ORDERS_TWO),
            (shares_one[0], swap(shares_one[1], "core"), ORDERS_ONE),
        )
    )
    names_two = list(zip(*(order for _, _, order in ORDERS_TWO)))
    names_one = list(zip(*(order for _, _, order in ORDERS_ONE)))
    results = []
    halos = swap_halos(*edges)
    for step in range(2):
        keeps, sends = add_terms(two)
        one, sends = fence(one, sends)
        two = swaps(keeps, sends, names_two[step])
        keeps, sends = add_terms(one)
        one = swaps(keeps, sends, names_one[step])
        results.append(finish(step, sends, halos))
        two, results[-1] = fence(two, results[-1])
    keeps, sends = add_terms(join(two))
    one, sends = fence(one, sends)
    two = swaps(keeps, sends, names_two[2][:1])
    keeps, sends = add_terms(join(one))
    two, sends = fence(two, sends)
    one = swaps(keeps, sends, names_one[2][:1])
    keeps, sends = add_terms(two)
    one, sends = fence(one, sends)
    two = swaps(keeps, sends, [LAST])
    keeps, sends = add_terms(one)
    one = swaps(keeps, sends, [LAST])
    return [[term[0] for term in part[0]] for part in (one, two)], results


def per_device(
    features, cotangent, neighbour_table, send_lists, block_counts, weight_one, weight_two
):
    blocks, channels = features.shape[1], features.shape[3]
    dp_size, slab_size = lax.axis_size("dp"), lax.axis_size("slab")
    edge = send_lists.shape[3]
    taps_in = weight_one.shape[0]
    factor = 1.0 / math.sqrt(dp_size * slab_size * blocks * 64)
    voxels = blocks * 64
    slots = blocks + 2 * edge + 1
    packed = slab_size if (dp_size, slab_size, channels) == (4, 8, 256) else 0

    def array(*shape, dtype=BF16):
        return jax.ShapeDtypeStruct(shape, dtype)

    if packed:
        shares = [array(16, taps_in // slab_size // 2, 128)] * 2
    else:
        shares = [array(taps_in, channels, dtype=F32)]
    edges = array(edge, ROWS, 2 * channels)
    table = neighbour_table.transpose(1, 0, 2)
    planes = pltpu.VMEM((4, slots, ROWS, channels), BF16)
    ends = pltpu.VMEM((2, slots, ROWS, channels), BF16)
    inner_shape = array(9, 4 * blocks * ROWS, channels)
    outer_shape = array(9, 2 * blocks * ROWS, channels)
    total = array(voxels, channels, dtype=F32)
    full = pltpu.VMEM((taps_in, channels) if packed else (8, channels), F32)
    sem = pltpu.SemaphoreType.DMA
    field = array(4, blocks, ROWS, channels)
    held = array(taps_in, channels)

    def scratch(shape):
        return pltpu.VMEM(shape.shape, shape.dtype)

    product = 2 * voxels * taps_in * channels
    around = array(4, slots, ROWS, channels)
    first, second, shift, source, source_other = call(
        pack_kernel,
        [edges, edges, array(16 * ROWS, 12 * ROWS), around, around],
        (send_lists, jnp.concatenate([features, cotangent])),
        "sh",
        [sem((2, 4))],
        limit=6,
    )
    got_first, got_second = swap_halos(first, second)
    inner, inner_other, before, held_one = call(
        inner_kernel,
        [inner_shape, inner_shape, total, held],
        (table, source, source_other, shift, weight_one),
        "svvvh",
        [sem((3,))],
        limit=INNER_LIMIT,
        flops=2 * product,
    )
    hidden, outer, outer_other, *shares_two = call(
        functools.partial(forward_kernel, packed, ORDERS_TWO),
        [field, outer_shape, outer_shape] + shares,
        (
            table,
            source,
            source_other,
            got_first,
            got_second,
            shift,
            held_one,
            inner,
            inner_other,
            before,
        ),
        "svvvvvvvvv",
        [ends, full],
        limit=FORWARD_LIMIT,
        flops=2 * product,
    )
    grad_hidden, first, second = call(
        middle_kernel,
        [field, edges, edges],
        (send_lists, inner_other, outer_other, weight_two, hidden),
        "svvvv",
        [scratch(total)],
        limit=4,
        flops=product,
    )
    shares_one = call(
        functools.partial(backward_kernel, packed, ORDERS_ONE),
        shares,
        (inner, outer, grad_hidden),
        "vvv",
        [full],
        limit=10,
        flops=product,
    )
    seconds = (
        (hidden, weight_two, features),
        (grad_hidden, weight_one, cotangent),
    )

    def finish(part, tokens, halos):
        got_first, got_second = halos
        source, weight, rows = seconds[part]
        (out,) = call(
            functools.partial(second_kernel, part, part == 1, len(tokens)),
            [array(*features.shape)],
            (
                table,
                block_counts,
                source,
                got_first,
                got_second,
                shift,
                weight,
                rows,
                *tokens,
            ),
            "ssvvvvva" + "a" * len(tokens),
            [
                planes,
                pltpu.VMEM((blocks, 64, channels), BF16),
                scratch(inner_shape),
                scratch(outer_shape),
                scratch(total),
                sem,
            ],
            limit=10,
            flops=SECOND_COST * product,
        )
        return out

    if packed:
        terms, (output, grad_features) = reduce_packed(
            shares_one, shares_two, (first, second), finish
        )
        out = array(channels // dp_size, taps_in // slab_size, dtype=F32)
        grad_one, grad_two = (
            call(functools.partial(unpack_kernel, factor), [out], pair, "vv")[0].T
            for pair in terms
        )
    else:
        halos = swap_halos(first, second)
        output, grad_features = finish(0, [], halos), finish(1, [], halos)
        grad_one, grad_two = (
            lax.psum_scatter(
                lax.psum_scatter(share, "slab", scatter_dimension=0, tiled=True),
                "dp",
                scatter_dimension=1,
                tiled=True,
            )
            * factor
            for (share,) in (shares_one, shares_two)
        )
    return (output, grad_features, grad_one, grad_two)


def solution(mesh):
    in_specs = (
        P("dp", "slab", None, None),
        P("dp", "slab", None, None),
        P("dp", "slab", None),
        P("dp", "slab", None, None),
        P("dp", "slab"),
        P(),
        P(),
    )
    out_specs = (
        P("dp", "slab", None, None),
        P("dp", "slab", None, None),
        P("slab", "dp"),
        P("slab", "dp"),
    )
    return jax.shard_map(
        per_device, mesh=mesh, in_specs=in_specs, out_specs=out_specs, check_vma=False
    )
```

```python
import functools
import math

import jax
import jax.numpy as jnp
from jax import lax
from jax.experimental import pallas as pl
from jax.experimental.pallas import tpu as pltpu
from jax.sharding import PartitionSpec as P

F32 = jnp.float32
BF16 = jnp.bfloat16
TAPS = 27
ROWS = 16
MIB = 2**20
SECOND_COST = 1
INNER_LIMIT = 42
FORWARD_LIMIT = 14
UNROLL = 5

ORDERS_ONE = (("z1", "y", "x"), ("y", "z1", "x")), (2, 3)
ORDERS_TWO = (("x", "y", "z1"), ("y", "x", "z1")), (3, 5)
LAST = "z2"


def shift_matrix():
    shape = (16 * ROWS, 12 * ROWS)
    row = lax.broadcasted_iota(jnp.int32, shape, 0)
    column = lax.broadcasted_iota(jnp.int32, shape, 1)
    shift = (row >> 4) & 7
    shift = jnp.where(shift >= 4, shift + 1, shift)
    across = jnp.where(shift >= 6, 2, jnp.where(shift >= 3, 1, 0))
    y = ((row >> 2) & 3) + across + 3
    z = (row & 3) + (shift - 3 * across) + 3
    own = jnp.where((y >> 2) == 1, 16, 0)
    source = 32 * (z >> 2) + own + 4 * (y & 3) + (z & 3)
    return jnp.where(column == source + 96 * (row >> 7), 1.0, 0.0).astype(BF16)


def portions_of(rows, plan):
    (order, other), (part, whole) = plan
    at = rows * part // whole // ROWS * ROWS
    return ((0, at, order), (at, rows, other))


def bit_of(name, dp_index, slab_index):
    if name == "y":
        return dp_index // 2
    if name == "x":
        return slab_index % 2
    if name == "z1":
        return slab_index // 2 % 2
    return slab_index // 4


def pair_perm(name, dp_size, slab_size):
    dp_flip = {"core": 1, "y": 2}.get(name, 0)
    slab_flip = {"x": 1, "z1": 2, "z2": 4}.get(name, 0)
    return [
        (d * slab_size + s, (d ^ dp_flip) * slab_size + (s ^ slab_flip))
        for d in range(dp_size)
        for s in range(slab_size)
    ]


def swap(array, name):
    dp_size, slab_size = lax.axis_size("dp"), lax.axis_size("slab")
    return lax.ppermute(array, ("dp", "slab"), pair_perm(name, dp_size, slab_size))


def swap_halos(first, second):
    count = lax.axis_size("slab")
    even = [(s, s ^ 1) for s in range(count) if s ^ 1 < count]
    odd = [(s, s + 1 if s % 2 else s - 1) for s in range(1, count) if s % 2 == 0 or s + 1 < count]
    return lax.ppermute(first, "slab", even), lax.ppermute(second, "slab", odd)


def pack_kernel(far_lists, fields, first, second, shift, planes, more, sems, lists, sem):
    blocks = fields.shape[1]
    copies = [pltpu.make_async_copy(far_lists, lists, sem)]
    copies[0].start()
    copies += start_planes(planes, fields.at[0:1], blocks, sems.at[0])
    copies += start_planes(more, fields.at[1:2], blocks, sems.at[1])
    shift[...] = shift_matrix()
    for field in (planes, more):
        field[:, blocks:] = jnp.zeros_like(field[:, blocks:])
    for copy in copies:
        copy.wait()
    pack_edges(lists, (planes, more), blocks, first, second)


def pack_edges(lists, fields, blocks, first, second):
    channels = fields[0].shape[3]
    odd = lax.rem(lax.axis_index("slab"), 2)
    for q in range(lists.shape[3]):
        for ref, side in ((first, 1 - odd), (second, odd)):
            block = lists[0, 0, side, q]
            inside = jnp.minimum(block, blocks - 1)
            for part, source in enumerate(fields):
                value = source[3 * side, inside]
                ref[q, :, part * channels : (part + 1) * channels] = jnp.where(
                    block < blocks, value, jnp.zeros_like(value)
                )


def start_planes(planes, source, blocks, sem):
    copies = []
    for x in range(4):
        if source.shape[2] != ROWS:
            piece = source.at[0, :, pl.ds(x * ROWS, ROWS), :]
        else:
            piece = source.at[x]
        copies.append(pltpu.make_async_copy(piece, planes.at[x, pl.ds(0, blocks)], sem.at[x]))
        copies[-1].start()
    return copies


def fill_edges(planes, blocks, got_first, got_second, lanes, places):
    edge = got_first.shape[0]
    planes[:, blocks:] = jnp.zeros_like(planes[:, blocks:])
    is_odd = lax.rem(lax.axis_index("slab"), 2) == 1
    for q in range(edge):
        one, two = got_first[q, :, lanes], got_second[q, :, lanes]
        planes[places[0], blocks + q] = jnp.where(is_odd, one, two)
        planes[places[1], blocks + edge + q] = jnp.where(is_odd, two, one)


def gather_shifts(shifted, planes, table, shift, blocks, wanted):
    matrix = shift[...]
    upper = lax.broadcasted_iota(jnp.int32, (ROWS, planes.shape[3]), 0) < 8

    def one_block(b, carry):
        for place in range(0, len(wanted), 2):
            stack, centres = [], []
            for at, slab in wanted[place : place + 2]:
                near_x = 0 if at == 0 else 2 if at == 5 else 1
                around = [planes[slab, table[b, 0, 9 * near_x + n]] for n in range(9)]
                for z in range(3):
                    stack += [jnp.where(upper, around[6 + z], around[z]), around[3 + z]]
                centres.append(around[4])
            moved = jnp.dot(
                matrix, jnp.concatenate(stack, axis=0), preferred_element_type=F32
            ).astype(BF16)
            for half in range(2):
                pieces = [
                    moved[(8 * half + n) * ROWS : (8 * half + n + 1) * ROWS] for n in range(8)
                ]
                pieces.insert(4, centres[half])
                for n, piece in enumerate(pieces):
                    start = (place + half) * blocks * ROWS + b * ROWS
                    shifted[n, pl.ds(pl.multiple_of(start, ROWS), ROWS), :] = piece
        return carry

    lax.fori_loop(0, blocks, one_block, 0, unroll=UNROLL)


INNER = ((1, 0), (2, 1), (3, 2), (4, 3))
OUTER = ((0, 0), (5, 1))


def inner_taps(inner, offset):
    step = inner.shape[1] // 4
    along_x, along_yz = offset // 9, offset % 9
    if along_x == 0:
        return inner[along_yz, : 3 * step, :], step
    return inner[along_yz, (along_x - 1) * step :, :], 0


def taps_of(inner, outer, offset):
    step = inner.shape[1] // 4
    along_x, along_yz = offset // 9, offset % 9
    own, _ = inner_taps(inner, offset)
    if along_x == 0:
        return jnp.concatenate([outer[along_yz, :step, :], own], axis=0)
    if along_x == 2:
        return jnp.concatenate([own, outer[along_yz, step:, :]], axis=0)
    return own


def tap_weight(weight, offset, flipped):
    channels = weight.shape[1]
    row = (TAPS - 1 - offset if flipped else offset) * channels
    return weight[row : row + channels, :]


def times(left, right, flipped):
    return lax.dot_general(
        left, right, (((1,), (1 if flipped else 0,)), ((), ())), preferred_element_type=F32
    )


def convolve(total, inner, outer, weight, flipped):
    order = list(range(9, 18)) + list(range(9)) + list(range(18, 27))
    for at, offset in enumerate(order):
        if outer is None:
            taps, first = inner_taps(inner, offset)
        else:
            taps, first = taps_of(inner, outer, offset), 0
        term = times(taps, tap_weight(weight, offset, flipped), flipped)
        if at == 0:
            total[...] = term
        else:
            total[first : first + term.shape[0], :] += term


def emit_share(grad, dest, portions, outs, tile_rows, slab_size):
    half = tile_rows // 2
    dp_index, slab_index = lax.axis_index("dp"), lax.axis_index("slab")
    core = lax.rem(dp_index, 2)
    lane = lax.broadcasted_iota(jnp.int32, (half, 128), 1)
    low = (lane < 64) == (core == 0)
    for y in range(2):
        upper = grad[dest * tile_rows : dest * tile_rows + half, y * 128 : (y + 1) * 128]
        lower = grad[dest * tile_rows + half : (dest + 1) * tile_rows, y * 128 : (y + 1) * 128]
        lower = pltpu.roll(lower, 64, 1)
        keep = jnp.where(low, upper, lower).astype(BF16)
        send = jnp.where(low, lower, upper).astype(BF16)
        keep_ref, send_ref = outs
        for first, last, order in portions:
            index = 0
            for name in order + (LAST,):
                bit = bit_of(name, dp_index, slab_index)
                mine = y if name == "y" else bit_of(name, 0, dest)
                index = index * 2 + (bit ^ mine)
            keep_ref[index, first:last] = keep[first:last]
            send_ref[index, first:last] = send[first:last]


def emit_gradient(product, grad, portions, outs, packed):
    channels = grad.shape[1]
    if not packed:
        for offset in range(TAPS):
            outs[0][offset * channels : (offset + 1) * channels, :] = product(offset)
        return
    slab_size = packed
    tile_rows = TAPS * channels // slab_size
    done = 0
    for offset in range(TAPS):
        grad[offset * channels : (offset + 1) * channels, :] = product(offset)
        while done < slab_size and (done + 1) * tile_rows <= (offset + 1) * channels:
            emit_share(grad, done, portions, outs, tile_rows, slab_size)
            done += 1


def over_voxels(left, right):
    return lax.dot_general(left, right, (((0,), (0,)), ((), ())), preferred_element_type=F32)


def inner_kernel(table, planes, more, shift, weight, inner, other, before, held, sem):
    blocks = before.shape[0] // 64
    third = weight.shape[0] // 3
    fetches = []
    for i in (1, 0, 2):
        rows = pl.ds(i * third, third)
        fetches.append(pltpu.make_async_copy(weight.at[rows], held.at[rows], sem.at[i]))
        fetches[-1].start()
    gather_shifts(inner, planes, table, shift, blocks, INNER)
    gather_shifts(other, more, table, shift, blocks, INNER)
    for fetch in fetches:
        fetch.wait()
    convolve(before, inner, None, held, False)


def forward_kernel(
    packed,
    portions,
    table,
    source,
    source_other,
    got_first,
    got_second,
    shift,
    weight,
    inner,
    other,
    before,
    hidden,
    outer,
    outer_other,
    *rest,
):
    *outs, planes, grad = rest
    blocks, channels = hidden.shape[1], hidden.shape[3]
    step = blocks * ROWS
    for part, (field, target) in enumerate(((source, outer), (source_other, outer_other))):
        planes[0] = field[3]
        planes[1] = field[0]
        fill_edges(
            planes, blocks, got_first, got_second, pl.ds(part * channels, channels), (0, 1)
        )
        gather_shifts(target, planes, table, shift, blocks, OUTER)
    for x in range(4):
        value = before[x * step : (x + 1) * step, :]
        if x in (0, 3):
            for n in range(9):
                taps = outer[n, :step, :] if x == 0 else outer[n, step:, :]
                value += times(taps, tap_weight(weight, n if x == 0 else 18 + n, False), False)
        hidden[x] = jnp.maximum(value, 0.0).astype(BF16).reshape(hidden.shape[1:])
    left = hidden[...].reshape(4 * step, channels)
    emit_gradient(
        lambda offset: over_voxels(left, taps_of(other, outer_other, TAPS - 1 - offset)),
        grad,
        portions,
        outs,
        packed,
    )


def middle_kernel(
    lists, inner, outer, weight, hidden, grad_hidden, first, second, total
):
    blocks, channels = hidden.shape[1], hidden.shape[3]
    convolve(total, inner, outer, weight, True)
    kept = jnp.where(hidden[...].reshape(total.shape).astype(F32) > 0, total[...], 0.0)
    grad_hidden[...] = kept.astype(BF16).reshape(grad_hidden.shape)
    pack_edges(lists, (hidden, grad_hidden), blocks, first, second)


def backward_kernel(packed, portions, inner, outer, grad_hidden, *rest):
    *outs, grad = rest
    blocks, channels = grad_hidden.shape[1], grad_hidden.shape[3]
    right = grad_hidden[...].reshape(blocks * 64, channels)
    emit_gradient(
        lambda offset: over_voxels(taps_of(inner, outer, offset), right),
        grad,
        portions,
        outs,
        packed,
    )


def second_kernel(
    part, flipped, tokens, table, counts, source, got_first, got_second, shift, weight, rows, *rest
):
    out, planes, own, inner, outer, total, sem = rest[tokens:]
    blocks, channels = rows.shape[1], rows.shape[3]
    later = pltpu.make_async_copy(rows.at[0], own, sem)
    later.start()
    planes[:, :blocks] = source[...]
    fill_edges(
        planes, blocks, got_first, got_second, pl.ds(part * channels, channels), (3, 0)
    )
    gather_shifts(inner, planes, table, shift, blocks, INNER)
    gather_shifts(outer, planes, table, shift, blocks, ((0, 3), (5, 0)))
    convolve(total, inner, outer, weight, flipped)
    later.wait()
    for b in range(blocks):
        present = (b < counts[0, 0]).astype(F32)
        for x in range(4):
            at = slice(x * ROWS, (x + 1) * ROWS)
            added = own[b, at, :].astype(F32)
            start = (x * blocks + b) * ROWS
            term = total[start : start + ROWS, :]
            value = (added + term) * present if flipped else added * present + term
            out[0, b, at, :] = value.astype(BF16)


def unpack_kernel(factor, keep, got, out):
    core = lax.rem(lax.axis_index("dp"), 2)
    columns = out.shape[0]
    whole = (keep[...].astype(F32) + got[...].astype(F32)) * factor
    whole = jnp.where(core == 0, whole, pltpu.roll(whole, columns, 1)).T
    out[...] = jnp.concatenate([whole[:columns], whole[columns:]], axis=1)


def call(kernel, outs, ins, places, scratch=(), limit=24, flops=0):
    spaces = {"s": pltpu.SMEM, "v": pltpu.VMEM, "a": pl.ANY, "h": pltpu.HBM}
    return pl.pallas_call(
        kernel,
        out_shape=outs,
        in_specs=[pl.BlockSpec(memory_space=spaces[place]) for place in places],
        out_specs=[pl.BlockSpec(memory_space=pltpu.VMEM) for _ in outs],
        scratch_shapes=list(scratch),
        compiler_params=pltpu.CompilerParams(vmem_limit_bytes=limit * MIB),
        cost_estimate=pl.CostEstimate(flops=flops, bytes_accessed=0, transcendentals=0),
    )(*ins)


def add_terms(parts):
    keeps, sends = [], []
    for keep, got in parts:
        half = keep.shape[0] // 2
        sends.append(keep[half:] + got[half:])
        keeps.append(keep[:half] + got[:half])
    return keeps, sends


def cut(parts, orders):
    ((keep, got),) = parts
    return [[keep[:, first:last], got[:, first:last]] for first, last, _ in orders]


def swaps(keeps, sends, names):
    return [[keep, swap(send, name)] for keep, send, name in zip(keeps, sends, names)]


def join(parts):
    return [[jnp.concatenate([part[i] for part in parts], axis=1) for i in range(2)]]


def fence(parts, others):
    keeps, others = lax.optimization_barrier(([keep for keep, _ in parts], others))
    return [[keep, got] for keep, (_, got) in zip(keeps, parts)], others


def reduce_packed(shares_one, shares_two, orders_one, orders_two, edges, finish):
    two, one = (
        [[shares[0], swap(shares[1], "core")]] for shares in (shares_two, shares_one)
    )
    names_two = list(zip(*(order for _, _, order in orders_two)))
    names_one = list(zip(*(order for _, _, order in orders_one)))
    results = []
    halos = swap_halos(*edges)
    for step in range(2):
        keeps, sends = add_terms(two if step else cut(two, orders_two))
        one, sends = fence(one, sends)
        two = swaps(keeps, sends, names_two[step])
        keeps, sends = add_terms(one if step else cut(one, orders_one))
        one = swaps(keeps, sends, names_one[step])
        results.append(finish(step, sends, halos))
        two, results[-1] = fence(two, results[-1])
    keeps, sends = add_terms(join(two))
    one, sends = fence(one, sends)
    two = swaps(keeps, sends, names_two[2][:1])
    keeps, sends = add_terms(join(one))
    two, sends = fence(two, sends)
    one = swaps(keeps, sends, names_one[2][:1])
    keeps, sends = add_terms(two)
    one, sends = fence(one, sends)
    two = swaps(keeps, sends, [LAST])
    keeps, sends = add_terms(one)
    one = swaps(keeps, sends, [LAST])
    return [[term[0] for term in part[0]] for part in (one, two)], results


def per_device(
    features, cotangent, neighbour_table, send_lists, block_counts, weight_one, weight_two
):
    blocks, channels = features.shape[1], features.shape[3]
    dp_size, slab_size = lax.axis_size("dp"), lax.axis_size("slab")
    edge = send_lists.shape[3]
    taps_in = weight_one.shape[0]
    factor = 1.0 / math.sqrt(dp_size * slab_size * blocks * 64)
    voxels = blocks * 64
    slots = blocks + 2 * edge + 1
    packed = slab_size if (dp_size, slab_size, channels) == (4, 8, 256) else 0

    def array(*shape, dtype=BF16):
        return jax.ShapeDtypeStruct(shape, dtype)

    half = taps_in // slab_size // 2
    orders_one, orders_two = portions_of(half, ORDERS_ONE), portions_of(half, ORDERS_TWO)
    if packed:
        shares = [array(16, taps_in // slab_size // 2, 128)] * 2
    else:
        shares = [array(taps_in, channels, dtype=F32)]
    edges = array(edge, ROWS, 2 * channels)
    table = neighbour_table.transpose(1, 0, 2)
    planes = pltpu.VMEM((4, slots, ROWS, channels), BF16)
    ends = pltpu.VMEM((2, slots, ROWS, channels), BF16)
    inner_shape = array(9, 4 * blocks * ROWS, channels)
    outer_shape = array(9, 2 * blocks * ROWS, channels)
    total = array(voxels, channels, dtype=F32)
    full = pltpu.VMEM((taps_in, channels) if packed else (8, channels), F32)
    sem = pltpu.SemaphoreType.DMA
    field = array(4, blocks, ROWS, channels)
    held = array(taps_in, channels)

    def scratch(shape):
        return pltpu.VMEM(shape.shape, shape.dtype)

    product = 2 * voxels * taps_in * channels
    around = array(4, slots, ROWS, channels)
    first, second, shift, source, source_other = call(
        pack_kernel,
        [edges, edges, array(16 * ROWS, 12 * ROWS), around, around],
        (send_lists, jnp.concatenate([features, cotangent])),
        "hh",
        [sem((2, 4)), pltpu.SMEM(send_lists.shape, jnp.int32), sem],
        limit=6,
    )
    got_first, got_second = swap_halos(first, second)
    inner, inner_other, before, held_one = call(
        inner_kernel,
        [inner_shape, inner_shape, total, held],
        (table, source, source_other, shift, weight_one),
        "svvvh",
        [sem((3,))],
        limit=INNER_LIMIT,
        flops=2 * product,
    )
    hidden, outer, outer_other, *shares_two = call(
        functools.partial(forward_kernel, packed, orders_two),
        [field, outer_shape, outer_shape] + shares,
        (
            table,
            source,
            source_other,
            got_first,
            got_second,
            shift,
            held_one,
            inner,
            inner_other,
            before,
        ),
        "svvvvvvvvv",
        [ends, full],
        limit=FORWARD_LIMIT,
        flops=2 * product,
    )
    grad_hidden, first, second = call(
        middle_kernel,
        [field, edges, edges],
        (send_lists, inner_other, outer_other, weight_two, hidden),
        "svvvv",
        [scratch(total)],
        limit=4,
        flops=product,
    )
    shares_one = call(
        functools.partial(backward_kernel, packed, orders_one),
        shares,
        (inner, outer, grad_hidden),
        "vvv",
        [full],
        limit=10,
        flops=product,
    )
    seconds = (
        (hidden, weight_two, features),
        (grad_hidden, weight_one, cotangent),
    )

    def finish(part, tokens, halos):
        got_first, got_second = halos
        source, weight, rows = seconds[part]
        (out,) = call(
            functools.partial(second_kernel, part, part == 1, len(tokens)),
            [array(*features.shape)],
            (
                table,
                block_counts,
                source,
                got_first,
                got_second,
                shift,
                weight,
                rows,
                *tokens,
            ),
            "ssvvvvva" + "a" * len(tokens),
            [
                planes,
                pltpu.VMEM((blocks, 64, channels), BF16),
                scratch(inner_shape),
                scratch(outer_shape),
                scratch(total),
                sem,
            ],
            limit=10,
            flops=SECOND_COST * product,
        )
        return out

    if packed:
        terms, (output, grad_features) = reduce_packed(
            shares_one, shares_two, orders_one, orders_two, (first, second), finish
        )
        out = array(channels // dp_size, taps_in // slab_size, dtype=F32)
        grad_one, grad_two = (
            call(functools.partial(unpack_kernel, factor), [out], pair, "vv")[0].T
            for pair in terms
        )
    else:
        halos = swap_halos(first, second)
        output, grad_features = finish(0, [], halos), finish(1, [], halos)
        grad_one, grad_two = (
            lax.psum_scatter(
                lax.psum_scatter(share, "slab", scatter_dimension=0, tiled=True),
                "dp",
                scatter_dimension=1,
                tiled=True,
            )
            * factor
            for (share,) in (shares_one, shares_two)
        )
    return (output, grad_features, grad_one, grad_two)


def solution(mesh):
    in_specs = (
        P("dp", "slab", None, None),
        P("dp", "slab", None, None),
        P("dp", "slab", None),
        P("dp", "slab", None, None),
        P("dp", "slab"),
        P(),
        P(),
    )
    out_specs = (
        P("dp", "slab", None, None),
        P("dp", "slab", None, None),
        P("slab", "dp"),
        P("slab", "dp"),
    )
    return jax.shard_map(
        per_device, mesh=mesh, in_specs=in_specs, out_specs=out_specs, check_vma=False
    )
```
